32 devices in a mesh: groups: 2 (over y), sweep: 8 (over z, x), tile: 2 (over core).
Axes of the slice: x: 2, y: 2, z: 4, core: 2. Of those that a mesh axis runs over, the one named last changes fastest.
Arguments:
- point_feats: bfloat16 [524288, 128], P(('groups', 'sweep', 'tile')), parts along dimension 0, may hold values from -6 to 6
- cotangent: bfloat16 [294912, 128], P(('groups', 'sweep', 'tile')), parts along dimension 0, may hold values from -6 to 6
- send_index: int32 [32, 16, 512], P(('groups', 'sweep', 'tile')), parts along dimension 0, may hold values from 0 to 9215, as said below
- point_slot: int32 [524288], P(('groups', 'sweep', 'tile')), parts along dimension 0, may hold values from 0 to 8191, as said below
- live_count: int32 [32], P(('groups', 'sweep', 'tile')), parts along dimension 0, may hold values from 4096 to 16384
- inner_weight: bfloat16 [128, 128], replicated, may hold values from -0.5 to 0.5
- inner_bias: float32 [128], replicated, may hold values from -4 to 4
- outer_weight: bfloat16 [128, 128], replicated, may hold values from -0.5 to 0.5
- outer_bias: float32 [128], replicated, may hold values from -4 to 4
Outputs:
- point_grads: bfloat16 [524288, 128], P(('groups', 'sweep', 'tile')), parts along dimension 0
- inner_grad: float32 [256, 128], P('groups'), parts along dimension 0
- outer_grad: float32 [256, 128], P('groups'), parts along dimension 0
- ibias_grad: float32 [256], P('groups'), parts along dimension 0
- obias_grad: float32 [256], P('groups'), parts along dimension 0
The draws below stay inside these ranges and needn't reach their ends.
There are 2 independent parts, one for each index of `groups`. The reference program is written for one: setup_inputs(seed, part) draws one part's arguments, and reference() takes and returns one part's arrays. A program takes and returns all parts, laid end to end along the dimension named above; an argument that names none is the same for every part. Nothing has to cross between parts.
Inputs may be any that keep to these rules, and one draw needn't show every extreme that they name: send_index[r, d, j] is one of owner r's own 9216 cells, numbered locally; read as one list of 8192 entries per owner (d slowest), its aligned runs of 128 entries take run w's cells from w * 9216 * 256 // 16384 up to but not including (w + 1) * 9216 * 256 // 16384. point_slot on device d indexes the 8192 rows that d receives, owner by owner; the points of the aligned run b of 256 points of one device take rows from 128 * b up to but not including 128 * b + 128.
All inputs are finite; a program needn't handle non-finite values.
Results may differ from the reference program's by a relative error of at most 0.006.
Values may be sent and summed in bfloat16 or wider, within the bound.
A program may use at most 64 MiB of HBM per device.

```python
import math
import jax
import jax.numpy as jnp
from jax import lax

FEAT = 128
WIDTH = 128
CHANNELS = 128
TOK_DEV = 16384
CELL_DEV = 9216
OWNERS = 16
BLOCK = 512
POINTS = 262144
GRID = 147456
N_SWEEP = 8
N_TILE = 2


def draw_send_index(key, part):
    key = jax.random.fold_in(key, 11)
    window = CELL_DEV * 256 // TOK_DEV
    runs = OWNERS * BLOCK // 128
    local = jax.random.randint(key, (OWNERS, runs, 128), 0, window, dtype=jnp.int32)
    local = local.at[:, :, 0].set(0)
    local = local.at[:, :, 127].set(window - 1)
    starts = (jnp.arange(runs, dtype=jnp.int32) * window)[None, :, None]
    return (local + starts).reshape(OWNERS, OWNERS, BLOCK)


def draw_point_slot(key, part):
    key = jax.random.fold_in(key, 23)
    runs_dev = TOK_DEV // 256
    runs = OWNERS * runs_dev
    local = jax.random.randint(key, (runs, 256), 0, 128, dtype=jnp.int32)
    local = local.at[:, 0].set(0)
    local = local.at[:, 255].set(127)
    starts = (jnp.arange(runs, dtype=jnp.int32) % runs_dev * 128)[:, None]
    return (local + starts).reshape(OWNERS * TOK_DEV)


def with_ends(entries, own_key, least, largest):
    longest = entries.shape.index(max(entries.shape))
    spots = []
    for shift in (0, 1):
        where = [jax.random.randint(jax.random.fold_in(own_key, axis), (), 0, length) for axis, length in enumerate(entries.shape)]
        where[longest] = (where[longest] + shift) % entries.shape[longest]
        spots.append(tuple(where))
    return entries.at[spots[0]].set(least).at[spots[1]].set(largest)


def levels(stream_key, shape, shards, smallest, top_value):
    loudness = 1.0
    for dim, shards_of in shards:
        heights = jax.random.uniform(jax.random.fold_in(jax.random.fold_in(stream_key, 6), dim), (shards_of,), jnp.float32, smallest / len(shards), top_value / len(shards))
        loudness = loudness * jnp.repeat(jnp.exp(heights), shape[dim] // shards_of).reshape((-1,) + (1,) * (len(shape) - 1 - dim))
    return loudness


def normal_values(rng, dims, spread, bound, cuts=(), kind=jnp.bfloat16):
    drawn = spread * jax.random.normal(rng, dims, jnp.float32)
    if cuts:
        drawn = drawn * levels(rng, dims, cuts, -0.22, 0.18)
    return jnp.clip(drawn, -bound, bound).astype(kind)


def setup_inputs(seed: int = 0, part: int = 0) -> dict:
    key_list = jax.random.split(jax.random.key(seed), 10)
    part_splits = jax.random.split(jax.random.fold_in(key_list[9], part), 10)
    return {
        "point_feats": normal_values(part_splits[0], (POINTS, FEAT), 1.0, 6.0, ((0, 16),)),
        "cotangent": normal_values(part_splits[1], (GRID, CHANNELS), 1.0, 6.0, ((0, 16),)),
        "send_index": draw_send_index(jax.random.fold_in(jax.random.fold_in(key_list[9], part), 71), part),
        "point_slot": draw_point_slot(jax.random.fold_in(jax.random.fold_in(key_list[9], part), 71), part),
        "live_count": with_ends(jax.random.randint(part_splits[4], (OWNERS,), TOK_DEV // 4, TOK_DEV + 1), jax.random.fold_in(part_splits[4], 1), TOK_DEV // 4, TOK_DEV).astype(jnp.int32),
        "inner_weight": normal_values(key_list[5], (FEAT, WIDTH), FEAT ** -0.5, 0.5),
        "inner_bias": normal_values(key_list[6], (WIDTH,), 1.0, 4.0, (), jnp.float32),
        "outer_weight": normal_values(key_list[7], (WIDTH, CHANNELS), WIDTH ** -0.5, 0.5),
        "outer_bias": normal_values(key_list[8], (CHANNELS,), 1.0, 4.0, (), jnp.float32),
    }


def silu_slope(values):
    logistic = jax.nn.sigmoid(values)
    return logistic * (1.0 + values * (1.0 - logistic))

def rows_product(left, right):
    return lax.dot_general(left, right, (((0,), (0,)), ((), ())), preferred_element_type=jnp.float32)

def reference(point_feats, cotangent, send_index, point_slot, live_count, inner_weight, inner_bias, outer_weight, outer_bias):
    owners = N_SWEEP * N_TILE
    scaling = 1.0 / math.sqrt(POINTS)
    offsets = jnp.arange(TOK_DEV, dtype=jnp.int32)

    def one_device(carry, device):
        start = device * TOK_DEV
        feats = lax.dynamic_slice_in_dim(point_feats, start, TOK_DEV, 0)
        slots = lax.dynamic_slice_in_dim(point_slot, start, TOK_DEV, 0)
        table = lax.dynamic_index_in_dim(send_index, device, 1, keepdims=False)
        source = (slots // BLOCK).astype(jnp.int32)
        cells = table[source, slots % BLOCK] + source * CELL_DEV
        act_grad = jnp.take(cotangent, cells, axis=0)
        live_mask = offsets < live_count[device]
        act_grad = jnp.where(live_mask[:, None], act_grad, jnp.zeros_like(act_grad))
        pre_inner = jnp.dot(feats, inner_weight, preferred_element_type=jnp.float32) + inner_bias
        act_inner = jax.nn.silu(pre_inner).astype(jnp.bfloat16)
        pre_outer = jnp.dot(act_inner, outer_weight, preferred_element_type=jnp.float32) + outer_bias
        outer_delta = (act_grad.astype(jnp.float32) * silu_slope(pre_outer)).astype(jnp.bfloat16)
        outer_term = rows_product(act_inner, outer_delta)
        obias_term = lax.optimization_barrier(jnp.sum(outer_delta.astype(jnp.float32), axis=0))
        back_inner = jnp.dot(outer_delta, outer_weight.T, preferred_element_type=jnp.float32)
        inner_delta = (back_inner * silu_slope(pre_inner)).astype(jnp.bfloat16)
        inner_term = rows_product(feats, inner_delta)
        ibias_term = lax.optimization_barrier(jnp.sum(inner_delta.astype(jnp.float32), axis=0))
        grads = jnp.dot(inner_delta, inner_weight.T, preferred_element_type=jnp.float32).astype(jnp.bfloat16)
        totals = (carry[0] + inner_term, carry[1] + outer_term, carry[2] + ibias_term, carry[3] + obias_term)
        return (totals, grads)
    start_sums = (jnp.zeros((FEAT, WIDTH), jnp.float32), jnp.zeros((WIDTH, CHANNELS), jnp.float32), jnp.zeros((WIDTH,), jnp.float32), jnp.zeros((CHANNELS,), jnp.float32))
    totals, grads = lax.scan(one_device, start_sums, jnp.arange(owners, dtype=jnp.int32))
    point_grads = grads.reshape(POINTS, FEAT)
    return (point_grads, totals[0] * scaling, totals[1] * scaling, totals[2] * scaling, totals[3] * scaling)
```

```python
import functools
import math

import jax
import jax.numpy as jnp
from jax import lax
from jax.experimental import pallas as pl
from jax.experimental.pallas import tpu as pltpu
from jax.sharding import PartitionSpec as P

LANES = 128
RUN_POINTS = 256
CHUNK = 512


def transposed_dot(left, right):
    return lax.dot_general(
        left, right, (((0,), (0,)), ((), ())), preferred_element_type=jnp.float32
    )


def dot(left, right):
    return jnp.dot(left, right, preferred_element_type=jnp.float32)


def silu_parts(values):
    gate = 0.5 * jnp.tanh(0.5 * values) + 0.5
    act = values * gate
    return act, gate + act * (1.0 - gate)


def kernel(
    sweeps,
    tiles,
    scaling,
    live_ref,
    cot_ref,
    send_ref,
    slot_ref,
    inner_w_ref,
    inner_b_ref,
    outer_w_ref,
    outer_b_ref,
    feats_hbm,
    grads_hbm,
    inner_out,
    outer_out,
    bias_out,
    feats,
    outgoing,
    received,
    act_ref,
    inner_slope,
    outer_slope,
    picks,
    grads,
    inner_wt,
    outer_wt,
    inner_acc,
    outer_acc,
    bias_acc,
    terms,
    term_slots,
    totals,
    bias_term,
    bias_slots,
    feats_sem,
    grads_sem,
    row_send,
    row_recv,
    term_send,
    term_recv,
    bias_send,
    bias_recv,
    total_send,
    total_recv,
):
    owners = sweeps * tiles
    tok_rows = feats.shape[0]
    per_peer = outgoing.shape[0] // owners
    bits = owners.bit_length() - 1
    unit_peers = max(1, LANES // per_peer)
    unit_rows = unit_peers * per_peer
    unit_runs = unit_rows // LANES
    unit_points = unit_runs * RUN_POINTS
    units = owners // unit_peers
    window = cot_ref.shape[0] // (outgoing.shape[0] // LANES)
    share = terms.shape[1]
    feat = feats.shape[1]
    me = lax.axis_index("sweep") * tiles + lax.axis_index("tile")

    def paired(base, step):
        other = 0
        for bit in range(bits):
            scale = 1 << bit
            other = other + ((base // scale + step // scale) % 2) * scale
        return other

    def device(peer):
        return {"sweep": peer // tiles, "tile": peer % tiles}

    def far_near(turn):
        return (units - 1) - turn // 2 - (turn % 2) * (units // 2)

    load = pltpu.make_async_copy(feats_hbm, feats, feats_sem)
    load.start()

    barrier = pltpu.get_barrier_semaphore()

    def greet(step, carry):
        pl.semaphore_signal(
            barrier,
            inc=1,
            device_id=device(paired(me, step)),
            device_id_type=pl.DeviceIdType.MESH,
        )
        return carry

    lax.fori_loop(1, owners, greet, 0)

    def select(unit, target):
        for run in range(unit_runs):
            place = unit * unit_runs + run
            cells = send_ref[place] - place * window
            rows = lax.broadcasted_iota(jnp.int32, (window, LANES), 0)
            pick = jnp.where(rows == cells, 1.0, 0.0).astype(jnp.bfloat16)
            source = cot_ref[pl.ds(pl.multiple_of(place * window, 16), window), :]
            target[pl.ds(pl.multiple_of(place * LANES, LANES), LANES), :] = transposed_dot(
                pick, source
            ).astype(jnp.bfloat16)

    def row_copy(step, peer):
        return pltpu.make_async_remote_copy(
            src_ref=outgoing.at[pl.ds(pl.multiple_of(peer * per_peer, per_peer), per_peer)],
            dst_ref=received.at[pl.ds(pl.multiple_of(me * per_peer, per_peer), per_peer)],
            send_sem=row_send.at[step],
            recv_sem=row_recv.at[step],
            device_id=device(peer),
            device_id_type=pl.DeviceIdType.MESH,
        )

    my_unit = me // unit_peers

    def send_unit(turn, carry):
        unit_step = far_near(turn)
        select(paired(my_unit, unit_step), outgoing)
        for sub in range(unit_peers):
            step = unit_step * unit_peers + sub
            row_copy(step, paired(me, step)).start()
        return carry

    pl.semaphore_wait(barrier, owners - 1)
    lax.fori_loop(0, units - 1, send_unit, 0)
    select(my_unit, outgoing)
    own = pl.ds(pl.multiple_of(me * per_peer, per_peer), per_peer)
    received[own, :] = outgoing[own, :]
    for sub in range(1, unit_peers):
        row_copy(sub, paired(me, sub)).start()

    inner_wt[...] = inner_w_ref[...].T
    outer_wt[...] = outer_w_ref[...].T
    inner_acc[...] = jnp.zeros_like(inner_acc)
    outer_acc[...] = jnp.zeros_like(outer_acc)
    bias_acc[...] = jnp.zeros_like(bias_acc)
    live = live_ref[0]
    load.wait()

    def forward(chunk, carry):
        here = pl.ds(pl.multiple_of(chunk * CHUNK, CHUNK), CHUNK)
        act, slope = silu_parts(dot(feats[here, :], inner_w_ref[...]) + inner_b_ref[...])
        inner_slope[here, :] = slope
        act = act.astype(jnp.bfloat16)
        act_ref[here, :] = act
        _, slope = silu_parts(dot(act, outer_w_ref[...]) + outer_b_ref[...])
        outer_slope[here, :] = slope
        for part in range(CHUNK // LANES):
            line = chunk * (CHUNK // LANES) + part
            slots = slot_ref[line] - (line // (RUN_POINTS // LANES)) * LANES
            points = lax.broadcasted_iota(jnp.int32, (1, LANES), 1) + line * LANES
            slots = jnp.where(points < live, slots, -1)
            rows = lax.broadcasted_iota(jnp.int32, (LANES, LANES), 0)
            pick = jnp.where(rows == slots, 1.0, 0.0)
            picks[pl.ds(pl.multiple_of(line * LANES, LANES), LANES), :] = pick.T.astype(
                jnp.bfloat16
            )
        return carry

    lax.fori_loop(0, tok_rows // CHUNK, forward, 0)

    def out_copy(unit):
        place = pl.ds(pl.multiple_of(unit * unit_points, unit_points), unit_points)
        return pltpu.make_async_copy(grads.at[place], grads_hbm.at[place], grads_sem.at[unit])

    def backward(unit):
        outer_term = jnp.zeros(outer_acc.shape, jnp.float32)
        inner_term = jnp.zeros(inner_acc.shape, jnp.float32)
        outer_bias = jnp.zeros((8, LANES), jnp.float32)
        inner_bias = jnp.zeros((8, LANES), jnp.float32)
        for run in range(unit_runs):
            place = unit * unit_runs + run
            here = pl.ds(pl.multiple_of(place * RUN_POINTS, RUN_POINTS), RUN_POINTS)
            rows = received[pl.ds(pl.multiple_of(place * LANES, LANES), LANES), :]
            delta = (dot(picks[here, :], rows) * outer_slope[here, :]).astype(jnp.bfloat16)
            outer_term += transposed_dot(act_ref[here, :], delta)
            outer_bias += jnp.sum(delta.astype(jnp.float32).reshape(-1, 8, LANES), axis=0)
            delta = (dot(delta, outer_wt[...]) * inner_slope[here, :]).astype(jnp.bfloat16)
            inner_term += transposed_dot(feats[here, :], delta)
            inner_bias += jnp.sum(delta.astype(jnp.float32).reshape(-1, 8, LANES), axis=0)
            grads[here, :] = dot(delta, inner_wt[...]).astype(jnp.bfloat16)
        outer_acc[...] += outer_term
        inner_acc[...] += inner_term
        bias_acc[0] += inner_bias
        bias_acc[1] += outer_bias
        out_copy(unit).start()

    def arrived(unit_step, carry):
        for sub in range(unit_peers):
            step = unit_step * unit_peers + sub
            row_copy(step, paired(me, step)).wait_recv()
        backward(paired(my_unit, unit_step))
        return carry

    for sub in range(1, unit_peers):
        row_copy(sub, paired(me, sub)).wait_recv()
    backward(my_unit)
    lax.fori_loop(1, units // 2, arrived, 0)
    lax.fori_loop(0, units - units // 2, lambda turn, c: arrived(units - 1 - turn, c), 0)

    for place in range(owners):
        low = place * share
        if low < feat:
            terms[place] = inner_acc[low : low + share, :]
        else:
            terms[place] = outer_acc[low - feat : low - feat + share, :]
    bias_term[0:1, :] = jnp.sum(bias_acc[0], axis=0, keepdims=True)
    bias_term[1:2, :] = jnp.sum(bias_acc[1], axis=0, keepdims=True)

    def term_copy(step):
        peer = paired(me, step)
        return pltpu.make_async_remote_copy(
            src_ref=terms.at[peer],
            dst_ref=term_slots.at[me],
            send_sem=term_send.at[step],
            recv_sem=term_recv.at[step],
            device_id=device(peer),
            device_id_type=pl.DeviceIdType.MESH,
        )

    def bias_copy(step):
        return pltpu.make_async_remote_copy(
            src_ref=bias_term,
            dst_ref=bias_slots.at[me],
            send_sem=bias_send.at[step],
            recv_sem=bias_recv.at[step],
            device_id=device(paired(me, step)),
            device_id_type=pl.DeviceIdType.MESH,
        )

    def total_copy(step):
        return pltpu.make_async_remote_copy(
            src_ref=totals.at[me],
            dst_ref=totals.at[me],
            send_sem=total_send.at[step],
            recv_sem=total_recv.at[step],
            device_id=device(paired(me, step)),
            device_id_type=pl.DeviceIdType.MESH,
        )

    def each(act, first=1, last=None):
        def body(turn, carry):
            act(owners - turn)
            return carry

        lax.fori_loop(first, owners, body, 0)

    each(lambda step: term_copy(step).start())
    each(lambda step: bias_copy(step).start())
    term_slots[me] = terms[me]
    bias_slots[me] = bias_term[...]
    each(lambda step: term_copy(step).wait_recv())
    totals[me] = jnp.sum(term_slots[...], axis=0) * scaling
    each(lambda step: total_copy(step).start())
    each(lambda step: bias_copy(step).wait_recv())
    bias_out[...] = jnp.sum(bias_slots[...], axis=0) * scaling
    each(lambda step: row_copy(step, paired(me, step)).wait_send())
    each(lambda step: term_copy(step).wait_send())
    each(lambda step: bias_copy(step).wait_send())

    def drain(unit, carry):
        out_copy(unit).wait()
        return carry

    lax.fori_loop(0, units, drain, 0)
    each(lambda step: total_copy(step).wait_recv())
    for place in range(owners):
        low = place * share
        if low < feat:
            inner_out[low : low + share, :] = totals[place]
        else:
            outer_out[low - feat : low - feat + share, :] = totals[place]
    each(lambda step: total_copy(step).wait_send())


def local(
    point_feats,
    cotangent,
    send_index,
    point_slot,
    live_count,
    inner_weight,
    inner_bias,
    outer_weight,
    outer_bias,
):
    sweeps = lax.axis_size("sweep")
    tiles = lax.axis_size("tile")
    owners = sweeps * tiles
    tok_rows, feat = point_feats.shape
    width, channels = outer_weight.shape
    per_peer = send_index.shape[2]
    rows = owners * per_peer
    units = rows // max(per_peer, LANES)
    share = (feat + width) // owners
    scaling = 1.0 / math.sqrt(tok_rows * owners)
    vmem = pl.BlockSpec(memory_space=pltpu.VMEM)
    dma = pltpu.SemaphoreType.DMA
    half, full = jnp.bfloat16, jnp.float32
    flops = 2 * tok_rows * LANES * LANES * 8
    point_grads, inner_total, outer_total, biases = pl.pallas_call(
        functools.partial(kernel, sweeps, tiles, scaling),
        out_shape=(
            jax.ShapeDtypeStruct((tok_rows, feat), half),
            jax.ShapeDtypeStruct((feat, width), full),
            jax.ShapeDtypeStruct((width, channels), full),
            jax.ShapeDtypeStruct((2, width), full),
        ),
        in_specs=[pl.BlockSpec(memory_space=pltpu.SMEM)]
        + [vmem] * 7
        + [pl.BlockSpec(memory_space=pl.ANY)],
        out_specs=(pl.BlockSpec(memory_space=pl.ANY), vmem, vmem, vmem),
        scratch_shapes=[
            pltpu.VMEM((tok_rows, feat), half),
            pltpu.VMEM((rows, channels), half),
            pltpu.VMEM((rows, channels), half),
            pltpu.VMEM((tok_rows, width), half),
            pltpu.VMEM((tok_rows, width), full),
            pltpu.VMEM((tok_rows, channels), full),
            pltpu.VMEM((tok_rows, LANES), half),
            pltpu.VMEM((tok_rows, feat), half),
            pltpu.VMEM((width, feat), half),
            pltpu.VMEM((channels, width), half),
            pltpu.VMEM((feat, width), full),
            pltpu.VMEM((width, channels), full),
            pltpu.VMEM((2, 8, LANES), full),
            pltpu.VMEM((owners, share, LANES), full),
            pltpu.VMEM((owners, share, LANES), full),
            pltpu.VMEM((owners, share, LANES), full),
            pltpu.VMEM((2, LANES), full),
            pltpu.VMEM((owners, 2, LANES), full),
            dma(()),
            dma((units,)),
        ]
        + [dma((owners,))] * 8,
        compiler_params=pltpu.CompilerParams(
            collective_id=0, has_side_effects=True, vmem_limit_bytes=56 * 1024 * 1024
        ),
        cost_estimate=pl.CostEstimate(
            flops=flops, bytes_accessed=12 * 1024 * 1024, transcendentals=2 * tok_rows * LANES
        ),
        name="exchange",
    )(
        live_count,
        cotangent,
        send_index.reshape(-1, 1, LANES),
        point_slot.reshape(-1, 1, LANES),
        inner_weight,
        inner_bias.reshape(1, -1),
        outer_weight,
        outer_bias.reshape(1, -1),
        point_feats,
    )
    return point_grads, inner_total, outer_total, biases[0], biases[1]


def solution(mesh):
    placed = (
        P(("groups", "sweep", "tile"), None),
        P(("groups", "sweep", "tile"), None),
        P(("groups", "sweep", "tile"), None, None),
        P(("groups", "sweep", "tile")),
        P(("groups", "sweep", "tile")),
        P(),
        P(),
        P(),
        P(),
    )
    return jax.shard_map(
        local,
        mesh=mesh,
        in_specs=placed,
        out_specs=(
            P(("groups", "sweep", "tile"), None),
            P("groups", None),
            P("groups", None),
            P("groups"),
            P("groups"),
        ),
        check_vma=False,
    )
```

```python
import functools
import math

import jax
import jax.numpy as jnp
from jax import lax
from jax.experimental import pallas as pl
from jax.experimental.pallas import tpu as pltpu
from jax.sharding import PartitionSpec as P

LANES = 128
RUN_POINTS = 256
CHUNK = 512


def transposed_dot(left, right):
    return lax.dot_general(
        left, right, (((0,), (0,)), ((), ())), preferred_element_type=jnp.float32
    )


def dot(left, right):
    return jnp.dot(left, right, preferred_element_type=jnp.float32)


def silu_parts(values):
    gate = 0.5 * jnp.tanh(0.5 * values) + 0.5
    act = values * gate
    return act, gate + act * (1.0 - gate)


def kernel(
    sweeps,
    tiles,
    scaling,
    live_ref,
    cot_ref,
    send_ref,
    slot_ref,
    inner_w_ref,
    inner_b_ref,
    outer_w_ref,
    outer_b_ref,
    feats_hbm,
    grads,
    totals,
    bias_out,
    feats,
    outgoing,
    received,
    act_ref,
    inner_slope,
    outer_slope,
    picks,
    inner_wt,
    outer_wt,
    inner_acc,
    outer_acc,
    bias_acc,
    terms,
    term_slots,
    bias_term,
    bias_slots,
    index_rows,
    feats_sem,
    row_send,
    row_recv,
    term_send,
    term_recv,
    bias_send,
    bias_recv,
    total_send,
    total_recv,
):
    owners = sweeps * tiles
    tok_rows = feats.shape[0]
    per_peer = outgoing.shape[0] // owners
    bits = owners.bit_length() - 1
    unit_peers = max(1, LANES // per_peer)
    unit_rows = unit_peers * per_peer
    unit_runs = unit_rows // LANES
    units = owners // unit_peers
    window = cot_ref.shape[0] // (outgoing.shape[0] // LANES)
    share = terms.shape[1]
    feat = feats.shape[1]
    me = lax.axis_index("sweep") * tiles + lax.axis_index("tile")

    def paired(base, step):
        other = 0
        for bit in range(bits):
            scale = 1 << bit
            other = other + ((base // scale + step // scale) % 2) * scale
        return other

    def device(peer):
        return {"sweep": peer // tiles, "tile": peer % tiles}

    def far_near(turn):
        return (units - 1) - turn // 2 - (turn % 2) * (units // 2)

    load = pltpu.make_async_copy(feats_hbm, feats, feats_sem)
    load.start()

    barrier = pltpu.get_barrier_semaphore()

    def greet(step, carry):
        pl.semaphore_signal(
            barrier,
            inc=1,
            device_id=device(paired(me, step)),
            device_id_type=pl.DeviceIdType.MESH,
        )
        return carry

    lax.fori_loop(1, owners, greet, 0)

    for peer in range(owners):
        for low in range(0, per_peer, LANES):
            piece = min(per_peer, LANES)
            at = peer * per_peer + low
            index_rows[at // LANES, :, at % LANES : at % LANES + piece] = send_ref[
                0, peer : peer + 1, low : low + piece
            ]

    def select(unit, target):
        for run in range(unit_runs):
            place = unit * unit_runs + run
            cells = index_rows[place] - place * window
            rows = lax.broadcasted_iota(jnp.int32, (window, LANES), 0)
            pick = jnp.where(rows == cells, 1.0, 0.0).astype(jnp.bfloat16)
            source = cot_ref[pl.ds(pl.multiple_of(place * window, 16), window), :]
            target[pl.ds(pl.multiple_of(place * LANES, LANES), LANES), :] = transposed_dot(
                pick, source
            ).astype(jnp.bfloat16)

    def row_copy(step, peer):
        return pltpu.make_async_remote_copy(
            src_ref=outgoing.at[pl.ds(pl.multiple_of(peer * per_peer, per_peer), per_peer)],
            dst_ref=received.at[pl.ds(pl.multiple_of(me * per_peer, per_peer), per_peer)],
            send_sem=row_send.at[step],
            recv_sem=row_recv.at[step],
            device_id=device(peer),
            device_id_type=pl.DeviceIdType.MESH,
        )

    my_unit = me // unit_peers

    def send_unit(turn, carry):
        unit_step = far_near(turn)
        select(paired(my_unit, unit_step), outgoing)
        for sub in range(unit_peers):
            step = unit_step * unit_peers + sub
            row_copy(step, paired(me, step)).start()
        return carry

    pl.semaphore_wait(barrier, owners - 1)
    lax.fori_loop(0, units - 1, send_unit, 0)
    select(my_unit, outgoing)
    own = pl.ds(pl.multiple_of(me * per_peer, per_peer), per_peer)
    received[own, :] = outgoing[own, :]
    for sub in range(1, unit_peers):
        row_copy(sub, paired(me, sub)).start()

    inner_wt[...] = inner_w_ref[...].T
    outer_wt[...] = outer_w_ref[...].T
    inner_acc[...] = jnp.zeros_like(inner_acc)
    outer_acc[...] = jnp.zeros_like(outer_acc)
    bias_acc[...] = jnp.zeros_like(bias_acc)
    live = live_ref[0]
    load.wait()

    def forward(chunk, carry):
        here = pl.ds(pl.multiple_of(chunk * CHUNK, CHUNK), CHUNK)
        act, slope = silu_parts(dot(feats[here, :], inner_w_ref[...]) + inner_b_ref[...])
        inner_slope[here, :] = slope
        act = act.astype(jnp.bfloat16)
        act_ref[here, :] = act
        _, slope = silu_parts(dot(act, outer_w_ref[...]) + outer_b_ref[...])
        outer_slope[here, :] = slope
        for part in range(CHUNK // LANES):
            line = chunk * (CHUNK // LANES) + part
            slots = slot_ref[line] - (line // (RUN_POINTS // LANES)) * LANES
            points = lax.broadcasted_iota(jnp.int32, (1, LANES), 1) + line * LANES
            slots = jnp.where(points < live, slots, -1)
            rows = lax.broadcasted_iota(jnp.int32, (LANES, LANES), 0)
            pick = jnp.where(rows == slots, 1.0, 0.0)
            picks[pl.ds(pl.multiple_of(line * LANES, LANES), LANES), :] = pick.T.astype(
                jnp.bfloat16
            )
        return carry

    lax.fori_loop(0, tok_rows // CHUNK, forward, 0)

    def backward(unit):
        outer_term = jnp.zeros(outer_acc.shape, jnp.float32)
        inner_term = jnp.zeros(inner_acc.shape, jnp.float32)
        outer_bias = jnp.zeros((8, LANES), jnp.float32)
        inner_bias = jnp.zeros((8, LANES), jnp.float32)
        for run in range(unit_runs):
            place = unit * unit_runs + run
            here = pl.ds(pl.multiple_of(place * RUN_POINTS, RUN_POINTS), RUN_POINTS)
            rows = received[pl.ds(pl.multiple_of(place * LANES, LANES), LANES), :]
            delta = (dot(picks[here, :], rows) * outer_slope[here, :]).astype(jnp.bfloat16)
            outer_term += transposed_dot(act_ref[here, :], delta)
            outer_bias += jnp.sum(delta.astype(jnp.float32).reshape(-1, 8, LANES), axis=0)
            delta = (dot(delta, outer_wt[...]) * inner_slope[here, :]).astype(jnp.bfloat16)
            inner_term += transposed_dot(feats[here, :], delta)
            inner_bias += jnp.sum(delta.astype(jnp.float32).reshape(-1, 8, LANES), axis=0)
            grads[here, :] = dot(delta, inner_wt[...]).astype(jnp.bfloat16)
        outer_acc[...] += outer_term
        inner_acc[...] += inner_term
        bias_acc[0] += inner_bias
        bias_acc[1] += outer_bias

    def arrived(unit_step, carry):
        for sub in range(unit_peers):
            step = unit_step * unit_peers + sub
            row_copy(step, paired(me, step)).wait_recv()
        backward(paired(my_unit, unit_step))
        return carry

    for sub in range(1, unit_peers):
        row_copy(sub, paired(me, sub)).wait_recv()
    backward(my_unit)
    lax.fori_loop(1, units // 2, arrived, 0)
    lax.fori_loop(0, units - units // 2, lambda turn, c: arrived(units - 1 - turn, c), 0)

    for place in range(owners):
        low = place * share
        if low < feat:
            terms[place] = inner_acc[low : low + share, :]
        else:
            terms[place] = outer_acc[low - feat : low - feat + share, :]
    bias_term[0:1, :] = jnp.sum(bias_acc[0], axis=0, keepdims=True)
    bias_term[1:2, :] = jnp.sum(bias_acc[1], axis=0, keepdims=True)

    def term_copy(step):
        peer = paired(me, step)
        return pltpu.make_async_remote_copy(
            src_ref=terms.at[peer],
            dst_ref=term_slots.at[me],
            send_sem=term_send.at[step],
            recv_sem=term_recv.at[step],
            device_id=device(peer),
            device_id_type=pl.DeviceIdType.MESH,
        )

    def bias_copy(step):
        return pltpu.make_async_remote_copy(
            src_ref=bias_term,
            dst_ref=bias_slots.at[me],
            send_sem=bias_send.at[step],
            recv_sem=bias_recv.at[step],
            device_id=device(paired(me, step)),
            device_id_type=pl.DeviceIdType.MESH,
        )

    def total_copy(step):
        return pltpu.make_async_remote_copy(
            src_ref=totals.at[me],
            dst_ref=totals.at[me],
            send_sem=total_send.at[step],
            recv_sem=total_recv.at[step],
            device_id=device(paired(me, step)),
            device_id_type=pl.DeviceIdType.MESH,
        )

    def each(act, first=1, last=None):
        def body(turn, carry):
            act(owners - turn)
            return carry

        lax.fori_loop(first, owners, body, 0)

    each(lambda step: term_copy(step).start())
    each(lambda step: bias_copy(step).start())
    term_slots[me] = terms[me]
    bias_slots[me] = bias_term[...]
    each(lambda step: term_copy(step).wait_recv())
    totals[me] = jnp.sum(term_slots[...], axis=0) * scaling
    each(lambda step: total_copy(step).start())
    each(lambda step: bias_copy(step).wait_recv())
    bias_out[...] = jnp.sum(bias_slots[...], axis=0) * scaling
    each(lambda step: row_copy(step, paired(me, step)).wait_send())
    each(lambda step: term_copy(step).wait_send())
    each(lambda step: bias_copy(step).wait_send())

    each(lambda step: total_copy(step).wait_recv())
    each(lambda step: total_copy(step).wait_send())


def finish(
    grads_in, totals_in, biases_in, grads_out, inner_out, outer_out, ibias_out, obias_out, sems
):
    inner_parts = inner_out.shape[0] // totals_in.shape[1]
    outer_parts = totals_in.shape[0] - inner_parts
    copy = pltpu.make_async_copy(grads_in, grads_out, sems.at[0])
    copy.start()
    inner_out[...] = totals_in[:inner_parts].reshape(inner_out.shape)
    outer_out[...] = totals_in[inner_parts:].reshape(outer_out.shape)
    ibias_out[...] = biases_in[0]
    obias_out[...] = biases_in[1]
    copy.wait()


def local(
    point_feats,
    cotangent,
    send_index,
    point_slot,
    live_count,
    inner_weight,
    inner_bias,
    outer_weight,
    outer_bias,
):
    sweeps = lax.axis_size("sweep")
    tiles = lax.axis_size("tile")
    owners = sweeps * tiles
    tok_rows, feat = point_feats.shape
    width, channels = outer_weight.shape
    per_peer = send_index.shape[2]
    rows = owners * per_peer
    share = (feat + width) // owners
    scaling = 1.0 / math.sqrt(tok_rows * owners)
    vmem = pl.BlockSpec(memory_space=pltpu.VMEM)
    dma = pltpu.SemaphoreType.DMA
    half, full = jnp.bfloat16, jnp.float32
    flops = 2 * tok_rows * LANES * LANES * 8
    grads, totals, biases = pl.pallas_call(
        functools.partial(kernel, sweeps, tiles, scaling),
        out_shape=(
            pltpu.VMEM((tok_rows, feat), half),
            pltpu.VMEM((owners, share, LANES), full),
            pltpu.VMEM((2, width), full),
        ),
        in_specs=[pl.BlockSpec(memory_space=pltpu.SMEM)]
        + [vmem] * 7
        + [pl.BlockSpec(memory_space=pl.ANY)],
        out_specs=(vmem, vmem, vmem),
        scratch_shapes=[
            pltpu.VMEM((tok_rows, feat), half),
            pltpu.VMEM((rows, channels), half),
            pltpu.VMEM((rows, channels), half),
            pltpu.VMEM((tok_rows, width), half),
            pltpu.VMEM((tok_rows, width), full),
            pltpu.VMEM((tok_rows, channels), full),
            pltpu.VMEM((tok_rows, LANES), half),
            pltpu.VMEM((width, feat), half),
            pltpu.VMEM((channels, width), half),
            pltpu.VMEM((feat, width), full),
            pltpu.VMEM((width, channels), full),
            pltpu.VMEM((2, 8, LANES), full),
            pltpu.VMEM((owners, share, LANES), full),
            pltpu.VMEM((owners, share, LANES), full),
            pltpu.VMEM((2, LANES), full),
            pltpu.VMEM((owners, 2, LANES), full),
            pltpu.VMEM((rows // LANES, 1, LANES), jnp.int32),
            dma(()),
        ]
        + [dma((owners,))] * 8,
        compiler_params=pltpu.CompilerParams(
            collective_id=0, has_side_effects=True, vmem_limit_bytes=56 * 1024 * 1024
        ),
        cost_estimate=pl.CostEstimate(
            flops=flops, bytes_accessed=12 * 1024 * 1024, transcendentals=2 * tok_rows * LANES
        ),
        name="exchange",
    )(
        live_count,
        cotangent,
        send_index,
        point_slot.reshape(-1, 1, LANES),
        inner_weight,
        inner_bias.reshape(1, -1),
        outer_weight,
        outer_bias.reshape(1, -1),
        point_feats,
    )
    return pl.pallas_call(
        finish,
        out_shape=(
            jax.ShapeDtypeStruct((tok_rows, feat), half),
            jax.ShapeDtypeStruct((feat, width), full),
            jax.ShapeDtypeStruct((width, channels), full),
            jax.ShapeDtypeStruct((width,), full),
            jax.ShapeDtypeStruct((channels,), full),
        ),
        in_specs=[vmem, vmem, vmem],
        out_specs=(pl.BlockSpec(memory_space=pl.ANY), vmem, vmem, vmem, vmem),
        scratch_shapes=[dma((1,))],
        name="finish",
    )(grads, totals, biases)


def solution(mesh):
    placed = (
        P(("groups", "sweep", "tile"), None),
        P(("groups", "sweep", "tile"), None),
        P(("groups", "sweep", "tile"), None, None),
        P(("groups", "sweep", "tile")),
        P(("groups", "sweep", "tile")),
        P(),
        P(),
        P(),
        P(),
    )
    return jax.shard_map(
        local,
        mesh=mesh,
        in_specs=placed,
        out_specs=(
            P(("groups", "sweep", "tile"), None),
            P("groups", None),
            P("groups", None),
            P("groups"),
            P("groups"),
        ),
        check_vma=False,
    )
```

```python
import functools
import math

import jax
import jax.numpy as jnp
from jax import lax
from jax.experimental import pallas as pl
from jax.experimental.pallas import tpu as pltpu
from jax.sharding import PartitionSpec as P

LANES = 128
RUN_POINTS = 256
CHUNK = 512


def transposed_dot(left, right):
    return lax.dot_general(
        left, right, (((0,), (0,)), ((), ())), preferred_element_type=jnp.float32
    )


def dot(left, right):
    return jnp.dot(left, right, preferred_element_type=jnp.float32)


def silu_parts(values):
    gate = 0.5 * jnp.tanh(0.5 * values) + 0.5
    act = values * gate
    return act, gate + act * (1.0 - gate)


def kernel(
    sweeps,
    tiles,
    scaling,
    live_ref,
    send_ref,
    slot_ref,
    inner_w_ref,
    inner_b_ref,
    outer_w_ref,
    outer_b_ref,
    cot_hbm,
    feats_hbm,
    grads,
    totals,
    bias_out,
    feats,
    cot_ref,
    outgoing,
    received,
    act_ref,
    inner_slope,
    outer_slope,
    picks,
    inner_wt,
    outer_wt,
    inner_acc,
    outer_acc,
    bias_acc,
    terms,
    term_slots,
    bias_term,
    bias_slots,
    index_rows,
    feats_sem,
    cells_sem,
    row_send,
    row_recv,
    term_send,
    term_recv,
    bias_send,
    bias_recv,
    total_send,
    total_recv,
):
    owners = sweeps * tiles
    tok_rows = feats.shape[0]
    per_peer = outgoing.shape[0] // owners
    bits = owners.bit_length() - 1
    unit_peers = max(1, LANES // per_peer)
    unit_rows = unit_peers * per_peer
    unit_runs = unit_rows // LANES
    units = owners // unit_peers
    window = cot_ref.shape[0] // (outgoing.shape[0] // LANES)
    share = terms.shape[1]
    feat = feats.shape[1]
    me = lax.axis_index("sweep") * tiles + lax.axis_index("tile")

    flips = [(1 - 2 * ((me // (1 << bit)) % 2)) * (1 << bit) for bit in range(bits)]

    def paired(base, step):
        if isinstance(step, int):
            shift = bits - (units.bit_length() - 1) if base is not me else 0
            for bit in range(bits):
                if (step >> bit) & 1:
                    base = base + flips[bit + shift] // (1 << shift)
            return base
        other = 0
        for bit in range(bits):
            scale = 1 << bit
            other = other + ((base // scale + step // scale) % 2) * scale
        return other

    def device(peer):
        return {"sweep": peer // tiles, "tile": peer % tiles}

    def far_near(turn):
        return (units - 1) - turn // 2 - (turn % 2) * (units // 2)

    cells_load = pltpu.make_async_copy(cot_hbm, cot_ref, cells_sem)
    cells_load.start()
    load = pltpu.make_async_copy(feats_hbm, feats, feats_sem)
    load.start()

    barrier = pltpu.get_barrier_semaphore()

    for step in range(1, owners):
        pl.semaphore_signal(
            barrier,
            inc=1,
            device_id=device(paired(me, step)),
            device_id_type=pl.DeviceIdType.MESH,
        )

    for peer in range(owners):
        for low in range(0, per_peer, LANES):
            piece = min(per_peer, LANES)
            at = peer * per_peer + low
            index_rows[at // LANES, :, at % LANES : at % LANES + piece] = send_ref[
                0, peer : peer + 1, low : low + piece
            ]

    def select(unit, target):
        for run in range(unit_runs):
            place = unit * unit_runs + run
            cells = index_rows[place] - place * window
            rows = lax.broadcasted_iota(jnp.int32, (window, LANES), 0)
            pick = jnp.where(rows == cells, 1.0, 0.0).astype(jnp.bfloat16)
            source = cot_ref[pl.ds(pl.multiple_of(place * window, 16), window), :]
            target[pl.ds(pl.multiple_of(place * LANES, LANES), LANES), :] = transposed_dot(
                pick, source
            ).astype(jnp.bfloat16)

    def row_copy(step, peer):
        return pltpu.make_async_remote_copy(
            src_ref=outgoing.at[pl.ds(pl.multiple_of(peer * per_peer, per_peer), per_peer)],
            dst_ref=received.at[pl.ds(pl.multiple_of(me * per_peer, per_peer), per_peer)],
            send_sem=row_send.at[step],
            recv_sem=row_recv.at[step],
            device_id=device(peer),
            device_id_type=pl.DeviceIdType.MESH,
        )

    my_unit = me // unit_peers

    def send_unit(turn, carry):
        unit_step = far_near(turn)
        for sub in range(unit_peers):
            step = unit_step * unit_peers + sub
            row_copy(step, paired(me, step)).start()
        unit_step = (far_near(turn + 1) + units) % units
        select(paired(my_unit, unit_step), outgoing)
        return carry

    cells_load.wait()
    select(paired(my_unit, units - 1 + 0 * me), outgoing)
    pl.semaphore_wait(barrier, owners - 1)
    lax.fori_loop(0, units - 1, send_unit, 0)
    own = pl.ds(pl.multiple_of(me * per_peer, per_peer), per_peer)
    received[own, :] = outgoing[own, :]
    for sub in range(1, unit_peers):
        row_copy(sub, paired(me, sub)).start()

    inner_wt[...] = inner_w_ref[...].T
    outer_wt[...] = outer_w_ref[...].T
    inner_acc[...] = jnp.zeros_like(inner_acc)
    outer_acc[...] = jnp.zeros_like(outer_acc)
    bias_acc[...] = jnp.zeros_like(bias_acc)
    live = live_ref[0]
    load.wait()

    def forward(chunk, carry):
        here = pl.ds(pl.multiple_of(chunk * CHUNK, CHUNK), CHUNK)
        act, slope = silu_parts(dot(feats[here, :], inner_w_ref[...]) + inner_b_ref[...])
        inner_slope[here, :] = slope
        act = act.astype(jnp.bfloat16)
        act_ref[here, :] = act
        _, slope = silu_parts(dot(act, outer_w_ref[...]) + outer_b_ref[...])
        outer_slope[here, :] = slope
        for part in range(CHUNK // LANES):
            line = chunk * (CHUNK // LANES) + part
            slots = slot_ref[line] - (line // (RUN_POINTS // LANES)) * LANES
            points = lax.broadcasted_iota(jnp.int32, (1, LANES), 1) + line * LANES
            slots = jnp.where(points < live, slots, -1)
            rows = lax.broadcasted_iota(jnp.int32, (LANES, LANES), 0)
            pick = jnp.where(rows == slots, 1.0, 0.0)
            picks[pl.ds(pl.multiple_of(line * LANES, LANES), LANES), :] = pick.T.astype(
                jnp.bfloat16
            )
        return carry

    lax.fori_loop(0, tok_rows // CHUNK, forward, 0)

    def backward(unit):
        outer_term = jnp.zeros(outer_acc.shape, jnp.float32)
        inner_term = jnp.zeros(inner_acc.shape, jnp.float32)
        outer_bias = jnp.zeros((8, LANES), jnp.float32)
        inner_bias = jnp.zeros((8, LANES), jnp.float32)
        for run in range(unit_runs):
            place = unit * unit_runs + run
            here = pl.ds(pl.multiple_of(place * RUN_POINTS, RUN_POINTS), RUN_POINTS)
            rows = received[pl.ds(pl.multiple_of(place * LANES, LANES), LANES), :]
            delta = (dot(picks[here, :], rows) * outer_slope[here, :]).astype(jnp.bfloat16)
            outer_term += transposed_dot(act_ref[here, :], delta)
            outer_bias += jnp.sum(delta.astype(jnp.float32).reshape(-1, 8, LANES), axis=0)
            delta = (dot(delta, outer_wt[...]) * inner_slope[here, :]).astype(jnp.bfloat16)
            inner_term += transposed_dot(feats[here, :], delta)
            inner_bias += jnp.sum(delta.astype(jnp.float32).reshape(-1, 8, LANES), axis=0)
            grads[here, :] = dot(delta, inner_wt[...]).astype(jnp.bfloat16)
        outer_acc[...] += outer_term
        inner_acc[...] += inner_term
        bias_acc[0] += inner_bias
        bias_acc[1] += outer_bias

    def arrived(unit_step, carry):
        for sub in range(unit_peers):
            step = unit_step * unit_peers + sub
            row_copy(step, paired(me, step)).wait_recv()
        backward(paired(my_unit, unit_step))
        return carry

    for sub in range(1, unit_peers):
        row_copy(sub, paired(me, sub)).wait_recv()
    backward(my_unit)
    lax.fori_loop(1, units // 2, arrived, 0)
    lax.fori_loop(0, units - units // 2, lambda turn, c: arrived(units - 1 - turn, c), 0)

    for place in range(owners):
        low = place * share
        if low < feat:
            terms[place] = inner_acc[low : low + share, :]
        else:
            terms[place] = outer_acc[low - feat : low - feat + share, :]
    bias_term[0:1, :] = jnp.sum(bias_acc[0], axis=0, keepdims=True)
    bias_term[1:2, :] = jnp.sum(bias_acc[1], axis=0, keepdims=True)

    def term_copy(step):
        peer = paired(me, step)
        return pltpu.make_async_remote_copy(
            src_ref=terms.at[peer],
            dst_ref=term_slots.at[me],
            send_sem=term_send.at[step],
            recv_sem=term_recv.at[step],
            device_id=device(peer),
            device_id_type=pl.DeviceIdType.MESH,
        )

    def bias_copy(step):
        return pltpu.make_async_remote_copy(
            src_ref=bias_term,
            dst_ref=bias_slots.at[me],
            send_sem=bias_send.at[step],
            recv_sem=bias_recv.at[step],
            device_id=device(paired(me, step)),
            device_id_type=pl.DeviceIdType.MESH,
        )

    def total_copy(step):
        return pltpu.make_async_remote_copy(
            src_ref=totals.at[me],
            dst_ref=totals.at[me],
            send_sem=total_send.at[step],
            recv_sem=total_recv.at[step],
            device_id=device(paired(me, step)),
            device_id_type=pl.DeviceIdType.MESH,
        )

    def each(act):
        for step in range(owners - 1, 0, -1):
            act(step)

    each(lambda step: term_copy(step).start())
    each(lambda step: bias_copy(step).start())
    term_slots[me] = terms[me]
    bias_slots[me] = bias_term[...]
    each(lambda step: term_copy(step).wait_recv())
    totals[me] = (jnp.sum(term_slots[...], axis=0) * scaling).astype(totals.dtype)
    each(lambda step: total_copy(step).start())
    each(lambda step: bias_copy(step).wait_recv())
    bias_out[...] = jnp.sum(bias_slots[...], axis=0) * scaling
    each(lambda step: row_copy(step, paired(me, step)).wait_send())
    each(lambda step: term_copy(step).wait_send())
    each(lambda step: bias_copy(step).wait_send())

    each(lambda step: total_copy(step).wait_recv())
    each(lambda step: total_copy(step).wait_send())


def finish(
    grads_in,
    totals_in,
    biases_in,
    grads_out,
    inner_out,
    outer_out,
    ibias_out,
    obias_out,
    inner_full,
    outer_full,
    ibias_full,
    obias_full,
    sems,
):
    pieces = sems.shape[0] - 4
    rows = grads_in.shape[0] // pieces
    copies = []
    for piece in range(pieces):
        place = pl.ds(piece * rows, rows)
        copies.append(
            pltpu.make_async_copy(grads_in.at[place], grads_out.at[place], sems.at[piece])
        )
        copies[-1].start()
    inner_parts = inner_out.shape[0] // totals_in.shape[1]
    totals = totals_in[...].astype(jnp.float32)
    inner_full[...] = totals[:inner_parts].reshape(inner_out.shape)
    outer_full[...] = totals[inner_parts:].reshape(outer_out.shape)
    ibias_full[...] = biases_in[0]
    obias_full[...] = biases_in[1]
    outputs = (
        (inner_full, inner_out),
        (outer_full, outer_out),
        (ibias_full, ibias_out),
        (obias_full, obias_out),
    )
    for place, (held, out) in enumerate(outputs):
        copies.append(pltpu.make_async_copy(held, out, sems.at[pieces + place]))
        copies[-1].start()
    for copy in copies:
        copy.wait()


def local(
    point_feats,
    cotangent,
    send_index,
    point_slot,
    live_count,
    inner_weight,
    inner_bias,
    outer_weight,
    outer_bias,
):
    sweeps = lax.axis_size("sweep")
    tiles = lax.axis_size("tile")
    owners = sweeps * tiles
    tok_rows, feat = point_feats.shape
    width, channels = outer_weight.shape
    per_peer = send_index.shape[2]
    rows = owners * per_peer
    share = (feat + width) // owners
    scaling = 1.0 / math.sqrt(tok_rows * owners)
    vmem = pl.BlockSpec(memory_space=pltpu.VMEM)
    dma = pltpu.SemaphoreType.DMA
    half, full = jnp.bfloat16, jnp.float32
    flops = 2 * tok_rows * LANES * LANES * 8
    grads, totals, biases = pl.pallas_call(
        functools.partial(kernel, sweeps, tiles, scaling),
        out_shape=(
            pltpu.VMEM((tok_rows, feat), half),
            pltpu.VMEM((owners, share, LANES), half),
            pltpu.VMEM((2, width), full),
        ),
        in_specs=[pl.BlockSpec(memory_space=pltpu.SMEM)]
        + [vmem] * 6
        + [pl.BlockSpec(memory_space=pltpu.HBM)] * 2,
        out_specs=(vmem, vmem, vmem),
        scratch_shapes=[
            pltpu.VMEM((tok_rows, feat), half),
            pltpu.VMEM(cotangent.shape, half),
            pltpu.VMEM((rows, channels), half),
            pltpu.VMEM((rows, channels), half),
            pltpu.VMEM((tok_rows, width), half),
            pltpu.VMEM((tok_rows, width), full),
            pltpu.VMEM((tok_rows, channels), full),
            pltpu.VMEM((tok_rows, LANES), half),
            pltpu.VMEM((width, feat), half),
            pltpu.VMEM((channels, width), half),
            pltpu.VMEM((feat, width), full),
            pltpu.VMEM((width, channels), full),
            pltpu.VMEM((2, 8, LANES), full),
            pltpu.VMEM((owners, share, LANES), full),
            pltpu.VMEM((owners, share, LANES), full),
            pltpu.VMEM((2, LANES), full),
            pltpu.VMEM((owners, 2, LANES), full),
            pltpu.VMEM((rows // LANES, 1, LANES), jnp.int32),
            dma(()),
            dma(()),
        ]
        + [dma((owners,))] * 8,
        compiler_params=pltpu.CompilerParams(
            collective_id=0, has_side_effects=True, vmem_limit_bytes=57 * 1024 * 1024
        ),
        cost_estimate=pl.CostEstimate(
            flops=flops, bytes_accessed=12 * 1024 * 1024, transcendentals=2 * tok_rows * LANES
        ),
        name="exchange",
    )(
        live_count,
        send_index,
        point_slot.reshape(-1, 1, LANES),
        inner_weight,
        inner_bias.reshape(1, -1),
        outer_weight,
        outer_bias.reshape(1, -1),
        cotangent,
        point_feats,
    )
    return pl.pallas_call(
        finish,
        out_shape=(
            jax.ShapeDtypeStruct((tok_rows, feat), half),
            jax.ShapeDtypeStruct((feat, width), full),
            jax.ShapeDtypeStruct((width, channels), full),
            jax.ShapeDtypeStruct((width,), full),
            jax.ShapeDtypeStruct((channels,), full),
        ),
        in_specs=[vmem, vmem, vmem],
        out_specs=[pl.BlockSpec(memory_space=pl.ANY)] * 5,
        scratch_shapes=[
            pltpu.VMEM((feat, width), full),
            pltpu.VMEM((width, channels), full),
            pltpu.VMEM((width,), full),
            pltpu.VMEM((channels,), full),
            dma((8,)),
        ],
        compiler_params=pltpu.CompilerParams(vmem_limit_bytes=4 * 1024 * 1024),
        name="finish",
    )(*(pltpu.with_memory_space_constraint(x, pltpu.VMEM) for x in (grads, totals, biases)))


def solution(mesh):
    placed = (
        P(("groups", "sweep", "tile"), None),
        P(("groups", "sweep", "tile"), None),
        P(("groups", "sweep", "tile"), None, None),
        P(("groups", "sweep", "tile")),
        P(("groups", "sweep", "tile")),
        P(),
        P(),
        P(),
        P(),
    )
    return jax.shard_map(
        local,
        mesh=mesh,
        in_specs=placed,
        out_specs=(
            P(("groups", "sweep", "tile"), None),
            P("groups", None),
            P("groups", None),
            P("groups"),
            P("groups"),
        ),
        check_vma=False,
    )
```

```python
import functools
import math

import jax
import jax.numpy as jnp
from jax import lax
from jax.experimental import pallas as pl
from jax.experimental.pallas import tpu as pltpu
from jax.sharding import PartitionSpec as P

LANES = 128
RUN_POINTS = 256
CHUNK = 512


def transposed_dot(left, right):
    return lax.dot_general(
        left, right, (((0,), (0,)), ((), ())), preferred_element_type=jnp.float32
    )


def dot(left, right):
    return jnp.dot(left, right, preferred_element_type=jnp.float32)


def silu_parts(values):
    gate = 0.5 * jnp.tanh(0.5 * values) + 0.5
    act = values * gate
    return act, gate + act * (1.0 - gate)


def kernel(
    sweeps,
    tiles,
    scaling,
    live_ref,
    send_ref,
    slot_hbm,
    inner_w_hbm,
    inner_b_hbm,
    outer_w_hbm,
    outer_b_hbm,
    cot_hbm,
    feats_hbm,
    grads,
    totals,
    bias_out,
    feats,
    cot_ref,
    outgoing,
    received,
    act_ref,
    inner_slope,
    outer_slope,
    picks,
    inner_wt,
    outer_wt,
    inner_acc,
    outer_acc,
    bias_acc,
    terms,
    term_slots,
    bias_term,
    bias_slots,
    index_rows,
    slot_ref,
    inner_w_ref,
    inner_b_ref,
    outer_w_ref,
    outer_b_ref,
    side_sems,
    feats_sem,
    cells_sem,
    row_send,
    row_recv,
    term_send,
    term_recv,
    bias_send,
    bias_recv,
    total_send,
    total_recv,
):
    owners = sweeps * tiles
    tok_rows = feats.shape[0]
    per_peer = outgoing.shape[0] // owners
    bits = owners.bit_length() - 1
    unit_peers = max(1, LANES // per_peer)
    unit_rows = unit_peers * per_peer
    unit_runs = unit_rows // LANES
    units = owners // unit_peers
    window = cot_ref.shape[0] // (outgoing.shape[0] // LANES)
    share = terms.shape[1]
    feat = feats.shape[1]
    me = lax.axis_index("sweep") * tiles + lax.axis_index("tile")

    flips = [(1 - 2 * ((me // (1 << bit)) % 2)) * (1 << bit) for bit in range(bits)]

    def paired(base, step):
        if isinstance(step, int):
            shift = bits - (units.bit_length() - 1) if base is not me else 0
            for bit in range(bits):
                if (step >> bit) & 1:
                    base = base + flips[bit + shift] // (1 << shift)
            return base
        other = 0
        for bit in range(bits):
            scale = 1 << bit
            other = other + ((base // scale + step // scale) % 2) * scale
        return other

    def device(peer):
        return {"sweep": peer // tiles, "tile": peer % tiles}

    def far_near(turn):
        return (units - 1) - turn // 2 - (turn % 2) * (units // 2)

    cells_load = pltpu.make_async_copy(cot_hbm, cot_ref, cells_sem)
    cells_load.start()
    load = pltpu.make_async_copy(feats_hbm, feats, feats_sem)

    side_loads = [
        pltpu.make_async_copy(source, target, side_sems.at[place])
        for place, (source, target) in enumerate(
            (
                (slot_hbm, slot_ref),
                (inner_w_hbm, inner_w_ref),
                (inner_b_hbm, inner_b_ref),
                (outer_w_hbm, outer_w_ref),
                (outer_b_hbm, outer_b_ref),
            )
        )
    ]

    barrier = pltpu.get_barrier_semaphore()

    for step in range(1, owners):
        pl.semaphore_signal(
            barrier,
            inc=1,
            device_id=device(paired(me, step)),
            device_id_type=pl.DeviceIdType.MESH,
        )

    for peer in range(owners):
        for low in range(0, per_peer, LANES):
            piece = min(per_peer, LANES)
            at = peer * per_peer + low
            index_rows[at // LANES, :, at % LANES : at % LANES + piece] = send_ref[
                0, peer : peer + 1, low : low + piece
            ]

    def select(unit, target):
        for run in range(unit_runs):
            place = unit * unit_runs + run
            cells = index_rows[place] - place * window
            rows = lax.broadcasted_iota(jnp.int32, (window, LANES), 0)
            pick = jnp.where(rows == cells, 1.0, 0.0).astype(jnp.bfloat16)
            source = cot_ref[pl.ds(pl.multiple_of(place * window, 16), window), :]
            target[pl.ds(pl.multiple_of(place * LANES, LANES), LANES), :] = transposed_dot(
                pick, source
            ).astype(jnp.bfloat16)

    def row_copy(step, peer):
        return pltpu.make_async_remote_copy(
            src_ref=outgoing.at[pl.ds(pl.multiple_of(peer * per_peer, per_peer), per_peer)],
            dst_ref=received.at[pl.ds(pl.multiple_of(me * per_peer, per_peer), per_peer)],
            send_sem=row_send.at[step],
            recv_sem=row_recv.at[step],
            device_id=device(peer),
            device_id_type=pl.DeviceIdType.MESH,
        )

    my_unit = me // unit_peers

    def send_unit(turn, carry):
        unit_step = far_near(turn)
        for sub in range(unit_peers):
            step = unit_step * unit_peers + sub
            row_copy(step, paired(me, step)).start()
        unit_step = (far_near(turn + 1) + units) % units
        select(paired(my_unit, unit_step), outgoing)
        return carry

    cells_load.wait()
    load.start()
    for side in side_loads:
        side.start()
    select(paired(my_unit, units - 1 + 0 * me), outgoing)
    pl.semaphore_wait(barrier, owners - 1)
    lax.fori_loop(0, units - 1, send_unit, 0)
    own = pl.ds(pl.multiple_of(me * per_peer, per_peer), per_peer)
    received[own, :] = outgoing[own, :]
    for sub in range(1, unit_peers):
        row_copy(sub, paired(me, sub)).start()

    for side in side_loads:
        side.wait()
    inner_wt[...] = inner_w_ref[...].T
    outer_wt[...] = outer_w_ref[...].T
    inner_acc[...] = jnp.zeros_like(inner_acc)
    outer_acc[...] = jnp.zeros_like(outer_acc)
    bias_acc[...] = jnp.zeros_like(bias_acc)
    live = live_ref[0]
    load.wait()

    def forward(chunk, carry):
        here = pl.ds(pl.multiple_of(chunk * CHUNK, CHUNK), CHUNK)
        act, slope = silu_parts(dot(feats[here, :], inner_w_ref[...]) + inner_b_ref[...])
        inner_slope[here, :] = slope
        act = act.astype(jnp.bfloat16)
        act_ref[here, :] = act
        _, slope = silu_parts(dot(act, outer_w_ref[...]) + outer_b_ref[...])
        outer_slope[here, :] = slope
        for part in range(CHUNK // LANES):
            line = chunk * (CHUNK // LANES) + part
            slots = slot_ref[line] - (line // (RUN_POINTS // LANES)) * LANES
            points = lax.broadcasted_iota(jnp.int32, (1, LANES), 1) + line * LANES
            slots = jnp.where(points < live, slots, -1)
            rows = lax.broadcasted_iota(jnp.int32, (LANES, LANES), 0)
            pick = jnp.where(rows == slots, 1.0, 0.0)
            picks[pl.ds(pl.multiple_of(line * LANES, LANES), LANES), :] = pick.T.astype(
                jnp.bfloat16
            )
        return carry

    lax.fori_loop(0, tok_rows // CHUNK, forward, 0)

    def backward(unit):
        outer_term = jnp.zeros(outer_acc.shape, jnp.float32)
        inner_term = jnp.zeros(inner_acc.shape, jnp.float32)
        outer_bias = jnp.zeros((8, LANES), jnp.float32)
        inner_bias = jnp.zeros((8, LANES), jnp.float32)
        for run in range(unit_runs):
            place = unit * unit_runs + run
            here = pl.ds(pl.multiple_of(place * RUN_POINTS, RUN_POINTS), RUN_POINTS)
            rows = received[pl.ds(pl.multiple_of(place * LANES, LANES), LANES), :]
            delta = (dot(picks[here, :], rows) * outer_slope[here, :]).astype(jnp.bfloat16)
            outer_term += transposed_dot(act_ref[here, :], delta)
            outer_bias += jnp.sum(delta.astype(jnp.float32).reshape(-1, 8, LANES), axis=0)
            delta = (dot(delta, outer_wt[...]) * inner_slope[here, :]).astype(jnp.bfloat16)
            inner_term += transposed_dot(feats[here, :], delta)
            inner_bias += jnp.sum(delta.astype(jnp.float32).reshape(-1, 8, LANES), axis=0)
            grads[here, :] = dot(delta, inner_wt[...]).astype(jnp.bfloat16)
        outer_acc[...] += outer_term
        inner_acc[...] += inner_term
        bias_acc[0] += inner_bias
        bias_acc[1] += outer_bias

    def arrived(unit_step, carry):
        for sub in range(unit_peers):
            step = unit_step * unit_peers + sub
            row_copy(step, paired(me, step)).wait_recv()
        backward(paired(my_unit, unit_step))
        return carry

    for sub in range(1, unit_peers):
        row_copy(sub, paired(me, sub)).wait_recv()
    backward(my_unit)
    lax.fori_loop(1, units // 2, arrived, 0)
    lax.fori_loop(0, units - units // 2, lambda turn, c: arrived(units - 1 - turn, c), 0)

    for place in range(owners):
        low = place * share
        if low < feat:
            terms[place] = inner_acc[low : low + share, :]
        else:
            terms[place] = outer_acc[low - feat : low - feat + share, :]
    bias_term[0:1, :] = jnp.sum(bias_acc[0], axis=0, keepdims=True)
    bias_term[1:2, :] = jnp.sum(bias_acc[1], axis=0, keepdims=True)

    def term_copy(step):
        peer = paired(me, step)
        return pltpu.make_async_remote_copy(
            src_ref=terms.at[peer],
            dst_ref=term_slots.at[me],
            send_sem=term_send.at[step],
            recv_sem=term_recv.at[step],
            device_id=device(peer),
            device_id_type=pl.DeviceIdType.MESH,
        )

    def bias_copy(step):
        return pltpu.make_async_remote_copy(
            src_ref=bias_term,
            dst_ref=bias_slots.at[me],
            send_sem=bias_send.at[step],
            recv_sem=bias_recv.at[step],
            device_id=device(paired(me, step)),
            device_id_type=pl.DeviceIdType.MESH,
        )

    def total_copy(step):
        return pltpu.make_async_remote_copy(
            src_ref=totals.at[me],
            dst_ref=totals.at[me],
            send_sem=total_send.at[step],
            recv_sem=total_recv.at[step],
            device_id=device(paired(me, step)),
            device_id_type=pl.DeviceIdType.MESH,
        )

    def each(act):
        for step in range(owners - 1, 0, -1):
            act(step)

    each(lambda step: term_copy(step).start())
    each(lambda step: bias_copy(step).start())
    term_slots[me] = terms[me]
    bias_slots[me] = bias_term[...]
    each(lambda step: term_copy(step).wait_recv())
    totals[me] = (jnp.sum(term_slots[...], axis=0) * scaling).astype(totals.dtype)
    each(lambda step: total_copy(step).start())
    each(lambda step: bias_copy(step).wait_recv())
    bias_out[...] = jnp.sum(bias_slots[...], axis=0) * scaling
    each(lambda step: row_copy(step, paired(me, step)).wait_send())
    each(lambda step: term_copy(step).wait_send())
    each(lambda step: bias_copy(step).wait_send())

    each(lambda step: total_copy(step).wait_recv())
    each(lambda step: total_copy(step).wait_send())


def finish(
    grads_in,
    totals_in,
    biases_in,
    grads_out,
    inner_out,
    outer_out,
    ibias_out,
    obias_out,
    inner_full,
    outer_full,
    ibias_full,
    obias_full,
    sems,
):
    pieces = sems.shape[0] - 4
    rows = grads_in.shape[0] // pieces
    copies = []
    for piece in range(pieces):
        place = pl.ds(piece * rows, rows)
        copies.append(
            pltpu.make_async_copy(grads_in.at[place], grads_out.at[place], sems.at[piece])
        )
        copies[-1].start()
    inner_parts = inner_out.shape[0] // totals_in.shape[1]
    totals = totals_in[...].astype(jnp.float32)
    inner_full[...] = totals[:inner_parts].reshape(inner_out.shape)
    outer_full[...] = totals[inner_parts:].reshape(outer_out.shape)
    ibias_full[...] = biases_in[0]
    obias_full[...] = biases_in[1]
    outputs = (
        (inner_full, inner_out),
        (outer_full, outer_out),
        (ibias_full, ibias_out),
        (obias_full, obias_out),
    )
    for place, (held, out) in enumerate(outputs):
        copies.append(pltpu.make_async_copy(held, out, sems.at[pieces + place]))
        copies[-1].start()
    for copy in copies:
        copy.wait()


def local(
    point_feats,
    cotangent,
    send_index,
    point_slot,
    live_count,
    inner_weight,
    inner_bias,
    outer_weight,
    outer_bias,
):
    sweeps = lax.axis_size("sweep")
    tiles = lax.axis_size("tile")
    owners = sweeps * tiles
    tok_rows, feat = point_feats.shape
    width, channels = outer_weight.shape
    per_peer = send_index.shape[2]
    rows = owners * per_peer
    share = (feat + width) // owners
    scaling = 1.0 / math.sqrt(tok_rows * owners)
    vmem = pl.BlockSpec(memory_space=pltpu.VMEM)
    dma = pltpu.SemaphoreType.DMA
    half, full = jnp.bfloat16, jnp.float32
    flops = 2 * tok_rows * LANES * LANES * 8
    grads, totals, biases = pl.pallas_call(
        functools.partial(kernel, sweeps, tiles, scaling),
        out_shape=(
            pltpu.VMEM((tok_rows, feat), half),
            pltpu.VMEM((owners, share, LANES), half),
            pltpu.VMEM((2, width), full),
        ),
        in_specs=[pl.BlockSpec(memory_space=pltpu.SMEM)]
        + [vmem]
        + [pl.BlockSpec(memory_space=pltpu.HBM)] * 7,
        out_specs=(vmem, vmem, vmem),
        scratch_shapes=[
            pltpu.VMEM((tok_rows, feat), half),
            pltpu.VMEM(cotangent.shape, half),
            pltpu.VMEM((rows, channels), half),
            pltpu.VMEM((rows, channels), half),
            pltpu.VMEM((tok_rows, width), half),
            pltpu.VMEM((tok_rows, width), full),
            pltpu.VMEM((tok_rows, channels), full),
            pltpu.VMEM((tok_rows, LANES), half),
            pltpu.VMEM((width, feat), half),
            pltpu.VMEM((channels, width), half),
            pltpu.VMEM((feat, width), full),
            pltpu.VMEM((width, channels), full),
            pltpu.VMEM((2, 8, LANES), full),
            pltpu.VMEM((owners, share, LANES), full),
            pltpu.VMEM((owners, share, LANES), full),
            pltpu.VMEM((2, LANES), full),
            pltpu.VMEM((owners, 2, LANES), full),
            pltpu.VMEM((rows // LANES, 1, LANES), jnp.int32),
            pltpu.VMEM((tok_rows // LANES, 1, LANES), jnp.int32),
            pltpu.VMEM((feat, width), half),
            pltpu.VMEM((1, width), full),
            pltpu.VMEM((width, channels), half),
            pltpu.VMEM((1, channels), full),
            dma((5,)),
            dma(()),
            dma(()),
        ]
        + [dma((owners,))] * 8,
        compiler_params=pltpu.CompilerParams(
            collective_id=0, has_side_effects=True, vmem_limit_bytes=57 * 1024 * 1024
        ),
        cost_estimate=pl.CostEstimate(
            flops=flops, bytes_accessed=12 * 1024 * 1024, transcendentals=2 * tok_rows * LANES
        ),
        name="exchange",
    )(
        live_count,
        send_index,
        point_slot.reshape(-1, 1, LANES),
        inner_weight,
        inner_bias.reshape(1, -1),
        outer_weight,
        outer_bias.reshape(1, -1),
        cotangent,
        point_feats,
    )
    return pl.pallas_call(
        finish,
        out_shape=(
            jax.ShapeDtypeStruct((tok_rows, feat), half),
            jax.ShapeDtypeStruct((feat, width), full),
            jax.ShapeDtypeStruct((width, channels), full),
            jax.ShapeDtypeStruct((width,), full),
            jax.ShapeDtypeStruct((channels,), full),
        ),
        in_specs=[vmem, vmem, vmem],
        out_specs=[pl.BlockSpec(memory_space=pl.ANY)] * 5,
        scratch_shapes=[
            pltpu.VMEM((feat, width), full),
            pltpu.VMEM((width, channels), full),
            pltpu.VMEM((width,), full),
            pltpu.VMEM((channels,), full),
            dma((8,)),
        ],
        compiler_params=pltpu.CompilerParams(vmem_limit_bytes=4 * 1024 * 1024),
        name="finish",
    )(*(pltpu.with_memory_space_constraint(x, pltpu.VMEM) for x in (grads, totals, biases)))


def solution(mesh):
    placed = (
        P(("groups", "sweep", "tile"), None),
        P(("groups", "sweep", "tile"), None),
        P(("groups", "sweep", "tile"), None, None),
        P(("groups", "sweep", "tile")),
        P(("groups", "sweep", "tile")),
        P(),
        P(),
        P(),
        P(),
    )
    return jax.shard_map(
        local,
        mesh=mesh,
        in_specs=placed,
        out_specs=(
            P(("groups", "sweep", "tile"), None),
            P("groups", None),
            P("groups", None),
            P("groups"),
            P("groups"),
        ),
        check_vma=False,
    )
```
